128 devices in a mesh: row: 8 (over z, y_lo), col: 16 (over x, y_hi, core).
Axes of the slice: x: 4, y: 4 (y_hi: 2, y_lo: 2; y = y_hi * 2 + y_lo), z: 4, core: 2. Of those that a mesh axis runs over, the one named last changes fastest.
Arguments:
- inverse_anc: bfloat16 [16384, 16384], P('row', 'col'), may hold values from -6 to 6
- factor_panel: bfloat16 [16384, 4096], P('row', 'col'), may hold values from -0.046875 to 0.046875
- pattern: int32 [16, 64], replicated, may hold values 0 or 1
- diag_inverse: float32 [16, 256, 256], P('col'), may hold values from -6 to 6
Outputs:
- upper: bfloat16 [4096, 16384], P('col', 'row')
- diag_block: float32 [16, 256, 256], P('col')
The draws below stay inside these ranges and needn't reach their ends.
All inputs are finite; a program needn't handle non-finite values.
Results may differ from the reference program's by a relative error of at most 0.0095.
Values may be sent and summed in bfloat16 or wider, within the bound.
A program may use at most 192 MiB of HBM per device.

```python
import jax
import jax.numpy as jnp
from jax import lax

SUPER = 256
ANC_BLOCKS = 64
ANC_ROWS = 16384
LEAVES = 16
LEAF_COLS = 4096


def place_ends(values, stream_key, smallest, top_value):
    place = [jax.random.randint(jax.random.fold_in(stream_key, axis), (), 0, length) for axis, length in enumerate(values.shape)]
    main_axis = values.shape.index(max(values.shape))
    next_to = place[:main_axis] + [(place[main_axis] + 1) % values.shape[main_axis]] + place[main_axis + 1:]
    return values.at[tuple(place)].set(smallest).at[tuple(next_to)].set(top_value)


def level_of(rng, shape, shards, least, largest):
    def one(axis_at, shards_of):
        heights = jax.random.uniform(jax.random.fold_in(jax.random.fold_in(rng, 6), axis_at), (shards_of,), jnp.float32, least / len(shards), largest / len(shards))
        return jnp.repeat(jnp.exp(heights), shape[axis_at] // shards_of).reshape((-1,) + (1,) * (len(shape) - axis_at - 1))

    loudness = one(*shards[0])
    for cut in shards[1:]:
        loudness = loudness * one(*cut)
    return loudness


def bell_draw(rng, extent, width, reach, cuts=(), held_as=jnp.bfloat16):
    drawn = width * jax.random.normal(rng, extent, jnp.float32)
    if cuts:
        drawn = drawn * level_of(rng, extent, cuts, -0.22, 0.18)
    return jnp.clip(drawn, -reach, reach).astype(held_as)


def setup_inputs(seed: int = 0) -> dict:
    key_list = jax.random.split(jax.random.key(seed), 5)
    inverse_anc = bell_draw(key_list[0], (ANC_ROWS, ANC_ROWS), 1.0, 6.0, ((0, 8), (1, 16)))
    factor_panel = bell_draw(key_list[1], (ANC_ROWS, LEAF_COLS), ANC_ROWS ** -0.5, 0.046875, ((0, 8), (1, 16)))
    pattern = place_ends((jax.random.randint(key_list[2], (LEAVES, ANC_BLOCKS), 0, 2) < 1).astype(jnp.int32), jax.random.fold_in(key_list[2], 1), 0, 1)
    diag_inverse = bell_draw(key_list[3], (LEAVES, SUPER, SUPER), 1.0, 6.0, ((0, 16),), jnp.float32)
    return dict(inverse_anc=inverse_anc, factor_panel=factor_panel, pattern=pattern, diag_inverse=diag_inverse)


def reference(inverse_anc, factor_panel, pattern, diag_inverse):
    block_mask = jnp.repeat(jnp.repeat(pattern, SUPER, axis=0), SUPER, axis=1)
    masked = (factor_panel * block_mask.T.astype(jnp.bfloat16)).astype(jnp.bfloat16)
    product = lax.dot_general(masked.astype(jnp.float32), inverse_anc.astype(jnp.float32), (((0,), (1,)), ((), ())), precision=lax.Precision.HIGHEST)
    upper = (-product * block_mask.astype(jnp.float32)).astype(jnp.bfloat16)
    left = masked.astype(jnp.float32).reshape(ANC_ROWS, LEAVES, SUPER)
    right = upper.astype(jnp.float32).reshape(LEAVES, SUPER, ANC_ROWS)
    correction = jnp.einsum("akw,kva->kwv", left, right, precision=lax.Precision.HIGHEST)
    return upper, diag_inverse - correction
```

```python
import functools

import jax
import jax.numpy as jnp
from jax import lax
from jax.experimental import pallas as pl
from jax.experimental.pallas import tpu as pltpu
from jax.sharding import PartitionSpec as P

SUPER = 256
ROWS = 2048
HALF = 1024
NSUB = 16
SUB = 128
CH = 32
HC = 16
TILE = 256
BF = jnp.bfloat16
F32 = jnp.float32
MESH = pl.DeviceIdType.MESH

ORDER = [
    (0, 0, 0), (0, 0, 1),
    (1, 0, 0), (2, 0, 0), (0, 1, 0),
    (1, 0, 1), (2, 0, 1), (0, 1, 1),
    (3, 0, 0), (1, 1, 0), (2, 1, 0), (3, 1, 0),
    (3, 0, 1), (1, 1, 1), (2, 1, 1), (3, 1, 1),
]
BATCHES = [(0, 1), (1, 1), (2, 3), (5, 3), (8, 1), (9, 3), (12, 1), (13, 3)]
ZOFF = {0: 0, 1: 3, 2: 1, 3: 2}


def kernel(
    a_ref, f_ref, pat_ref, dinv_ref,
    u_ref, diag_ref,
    afull, mt, mask, tz, m, p, pown, ra, rb, da, db, ea, eb, s2, ysend, yrecv, dsend, drecv, dfin,
    a_sem, tz_s, tz_r, tx_s, tx_r, m_s, m_r, rs_s, rs_r, y_s, y_r, d_s, d_r,
):
    row = lax.axis_index("row")
    col = lax.axis_index("col")
    z, yl = row // 2, row % 2
    x, yh, h = col // 4, (col // 2) % 2, col % 2

    def dev(z=z, yl=yl, x=x, yh=yh, h=h):
        return (z * 2 + yl, (x * 2 + yh) * 2 + h)

    def remote(src, dst, ssem, rsem, to):
        return pltpu.make_async_remote_copy(
            src_ref=src, dst_ref=dst, send_sem=ssem, recv_sem=rsem, device_id=to, device_id_type=MESH
        )

    def arrive(ref, sem):
        pltpu.make_async_copy(ref, ref, sem).wait()

    sends = []

    def send(src, dst, ssem, rsem, to):
        copy = remote(src, dst, ssem, rsem, to)
        copy.start()
        sends.append(copy)

    zp, zm = (z + 1) % 4, (z + 3) % 4
    xp, xm = (x + 1) % 4, (x + 3) % 4

    barrier = pltpu.get_barrier_semaphore()
    partners = [dev(h=1 - h), dev(yh=1 - yh)]
    for dz in range(4):
        for fl in range(2):
            if dz or fl:
                partners.append(dev(z=(z + dz) % 4, yl=(yl + fl) % 2))
    for dx in range(4):
        for fl in range(2):
            if dx or fl:
                partners.append(dev(x=(x + dx) % 4, yl=(yl + fl) % 2, yh=(yh + fl) % 2))
    for to in partners:
        pl.semaphore_signal(barrier, inc=1, device_id=to, device_id_type=MESH)

    a_local = pltpu.make_async_copy(a_ref, afull.at[h], a_sem.at[0])
    a_local.start()

    for b in range(8):
        keep = pat_ref[col, row * 8 + b].astype(F32)
        mask[:, b * 256:(b + 1) * 256] = jnp.full((8, 256), keep, F32)
        block = f_ref[b * 256:(b + 1) * 256, :].astype(F32)
        mt[:, b * 256:(b + 1) * 256] = (block.T * keep).astype(BF)

    pl.semaphore_wait(barrier, len(partners))

    def piece(zz, g):
        return mt.at[pl.ds(pl.multiple_of(zz * 64 + g * CH, CH), CH)]

    for dz in (1, 3, 2):
        zz = (z + dz) % 4
        k = (4 - dz) % 4
        send(piece(zz, 0), tz.at[0, k], tz_s.at[0, k], tz_r.at[0, k], dev(z=zz))
    for dz in (0, 1, 3, 2):
        zz = (z + dz) % 4
        k = (4 - dz) % 4
        send(piece(zz, 1), tz.at[1, k], tz_s.at[1, k], tz_r.at[1, k], dev(z=zz, yl=1 - yl))
    send(a_ref, afull.at[h], a_sem.at[1], a_sem.at[2], dev(h=1 - h))

    tx_waits = []
    for g in range(2):
        nyh, nyl = (yl, yh) if g == 0 else (1 - yl, 1 - yh)
        same_y = yl == yh if g == 0 else yl != yh
        for k in (0, 1, 3, 2):
            if g == 0 and k == 0:
                src = piece(z, 0)
            else:
                src = tz.at[g, k]
                arrive(src, tz_r.at[g, k])
            xd = (z + k) % 4
            slot = (x + 4 - xd) % 4
            dst = m.at[pl.ds(pl.multiple_of(g * SUB + slot * CH, CH), CH)]
            far = remote(src, dst, tx_s.at[g, k], tx_r.at[g], dev(x=xd, yh=nyh, yl=nyl))
            near = pltpu.make_async_copy(src, dst, tx_r.at[g])
            here = jnp.logical_and(same_y, xd == x)

            @pl.when(here)
            def _():
                near.start()

            @pl.when(jnp.logical_not(here))
            def _():
                far.start()

            tx_waits.append((here, far))

    def msub(s, lo=0, n=SUB):
        return m.at[s * SUB + lo:s * SUB + lo + n]

    def multiply(s0, n):
        rows = slice(s0 * SUB, (s0 + n) * SUB)

        def tile(it, carry):
            at = pl.ds(pl.multiple_of(it * TILE, TILE), TILE)
            dims = (((1,), (1,)), ((), ()))
            acc = lax.dot_general(m[rows, :HALF], afull[0, at, :], dims, preferred_element_type=F32)
            acc += lax.dot_general(m[rows, HALF:], afull[1, at, :], dims, preferred_element_type=F32)
            for i in range(n):
                pown[s0 + i, :, at] = acc[i * SUB:i * SUB + CH]
                p[s0 + i, :, at] = acc[i * SUB + CH:(i + 1) * SUB].astype(BF)
            return carry

        lax.fori_loop(0, ROWS // TILE, tile, 0)

    def reduce_1(s):
        send(p.at[s, 32:48], ra.at[s], rs_s.at[s, 0], rs_r.at[s, 0], dev(x=xp))
        send(p.at[s, 48:64], rb.at[s], rs_s.at[s, 1], rs_r.at[s, 1], dev(x=xm))
        send(p.at[s, 16:32], db.at[s], rs_s.at[s, 2], rs_r.at[s, 2], dev(x=xp))
        send(p.at[s, 64:80], da.at[s], rs_s.at[s, 3], rs_r.at[s, 3], dev(x=xm))

    def reduce_2(s):
        arrive(ra.at[s], rs_r.at[s, 0])
        p[s, 0:16] = (p[s, 0:16].astype(F32) + ra[s].astype(F32)).astype(BF)
        send(p.at[s, 0:16], ea.at[s], rs_s.at[s, 4], rs_r.at[s, 4], dev(x=xp))
        arrive(rb.at[s], rs_r.at[s, 1])
        p[s, 80:96] = (p[s, 80:96].astype(F32) + rb[s].astype(F32)).astype(BF)
        send(p.at[s, 80:96], eb.at[s], rs_s.at[s, 5], rs_r.at[s, 5], dev(x=xm))

    def reduce_3(s):
        kind, fam, g = ORDER[s]
        arrive(db.at[s], rs_r.at[s, 2])
        arrive(da.at[s], rs_r.at[s, 3])
        arrive(ea.at[s], rs_r.at[s, 4])
        arrive(eb.at[s], rs_r.at[s, 5])
        pair = kind * 2 + g
        s2[pair, fam, 0:HC] = pown[s, 0:HC] + (ea[s].astype(F32) + da[s].astype(F32))
        s2[pair, fam, HC:CH] = pown[s, HC:CH] + (db[s].astype(F32) + eb[s].astype(F32))
        if fam == 1:
            mine = (yl + g + yh) % 2
            ysend[pair] = s2[pair, 1 - mine].astype(BF)
            send(ysend.at[pair], yrecv.at[pair], y_s.at[pair], y_r.at[pair], dev(yh=1 - yh))

    def finish(pair):
        kind, g = pair // 2, pair % 2
        mine = (yl + g + yh) % 2
        arrive(yrecv.at[pair], y_r.at[pair])
        total = s2[pair, mine] + yrecv[pair].astype(F32)
        zz = (z + ZOFF[kind]) % 4
        at = pl.ds(pl.multiple_of(zz * 64 + g * CH, CH), CH)
        u_ref[at, :] = (-total * mask[0:1, :]).astype(BF)

    def m_send(s, to, at, sem, lo=0, n=SUB):
        send(msub(s, lo, n), msub(at, lo, n), m_s.at[sem], m_r.at[sem], to)

    def on_arrival(b):
        if b == 0:
            arrive(msub(0), tx_r.at[0])
            m_send(0, dev(z=zp), 2, 2)
            m_send(0, dev(z=zm), 3, 3)
            m_send(0, dev(yl=1 - yl), 4, 4)
        elif b == 1:
            arrive(msub(1), tx_r.at[1])
            m_send(1, dev(z=zp), 5, 5)
            m_send(1, dev(z=zm), 6, 6)
            m_send(1, dev(yl=1 - yl), 7, 7)
        elif b in (2, 3):
            g = b - 2
            s0 = 2 + 3 * g
            for s in range(s0, s0 + 3):
                arrive(msub(s), m_r.at[s])
            m_send(s0, dev(z=zp), 8 + 4 * g, 8 + 4 * g, 0, 64)
            m_send(s0 + 1, dev(z=zm), 8 + 4 * g, 16 + g, 64, 64)
            m_send(s0 + 2, dev(z=zp), 9 + 4 * g, 9 + 4 * g)
            m_send(s0 + 2, dev(z=zm), 10 + 4 * g, 10 + 4 * g)
        elif b in (4, 6):
            g = (b - 4) // 2
            s = 8 + 4 * g
            arrive(msub(s, 0, 64), m_r.at[s])
            arrive(msub(s, 64, 64), m_r.at[16 + g])
            m_send(s, dev(yl=1 - yl), s + 3, s + 3)
        else:
            g = (b - 5) // 2
            for s in range(9 + 4 * g, 12 + 4 * g):
                arrive(msub(s), m_r.at[s])

    done = {}
    todo2, todo3 = [], []
    finished = []

    def run_3(s):
        reduce_3(s)
        kind, fam, g = ORDER[s]
        if fam == 1:
            finished.append(kind * 2 + g)

    for b, (s0, n) in enumerate(BATCHES):
        on_arrival(b)
        if b == 0:
            a_local.wait()
            arrive(afull.at[1 - h], a_sem.at[2])
        multiply(s0, n)
        for s in range(s0, s0 + n):
            reduce_1(s)
        for s in todo3:
            run_3(s)
        for s in todo2:
            reduce_2(s)
        todo3, todo2 = todo2, list(range(s0, s0 + n))
    for s in todo3:
        run_3(s)
    for s in todo2:
        reduce_2(s)
    for s in todo2:
        run_3(s)
    for pair in finished:
        finish(pair)

    corr = lax.dot_general(mt[...], u_ref[...], (((1,), (1,)), ((), ())), preferred_element_type=F32)
    dsend[...] = corr.astype(BF)

    def share(r):
        return pl.ds(pl.multiple_of(r * CH, CH), CH)

    def others():
        for k in range(1, 8):
            r = (row + k) % 8
            yield k, r, (r, col)

    for k, r, to in others():
        send(dsend.at[share(r)], drecv.at[8 - k], d_s.at[0, k], d_r.at[0, 8 - k], to)
    total = dsend[share(row), :].astype(F32)
    for k in range(1, 8):
        arrive(drecv.at[k], d_r.at[0, k])
        total += drecv[k].astype(F32)
    dfin[share(row), :] = total.astype(BF)
    for k, r, to in others():
        send(dfin.at[share(row)], dfin.at[share(row)], d_s.at[1, k], d_r.at[1, 8 - k], to)
    for k, r, to in others():
        arrive(dfin.at[share(r)], d_r.at[1, k])
    diag_ref[0] = dinv_ref[0] - dfin[...].astype(F32)

    for copy in sends:
        copy.wait_send()
    for here, far in tx_waits:
        @pl.when(jnp.logical_not(here))
        def _():
            far.wait_send()


def local(inverse_anc, factor_panel, pattern, diag_inverse):
    vmem = pl.BlockSpec(memory_space=pltpu.VMEM)
    dma = pltpu.SemaphoreType.DMA
    part = pltpu.VMEM((NSUB, HC, ROWS), BF)
    return pl.pallas_call(
        kernel,
        out_shape=(
            jax.ShapeDtypeStruct((SUPER, ROWS), BF),
            jax.ShapeDtypeStruct((1, SUPER, SUPER), F32),
        ),
        in_specs=[
            pl.BlockSpec(memory_space=pl.ANY),
            vmem,
            pl.BlockSpec(memory_space=pltpu.SMEM),
            vmem,
        ],
        out_specs=(vmem, vmem),
        scratch_shapes=[
            pltpu.VMEM((2, ROWS, HALF), BF),
            pltpu.VMEM((SUPER, ROWS), BF),
            pltpu.VMEM((8, ROWS), F32),
            pltpu.VMEM((2, 4, CH, ROWS), BF),
            pltpu.VMEM((NSUB * SUB, ROWS), BF),
            pltpu.VMEM((NSUB, 3 * CH, ROWS), BF),
            pltpu.VMEM((NSUB, CH, ROWS), F32),
            part, part, part, part, part, part,
            pltpu.VMEM((8, 2, CH, ROWS), F32),
            pltpu.VMEM((8, CH, ROWS), BF),
            pltpu.VMEM((8, CH, ROWS), BF),
            pltpu.VMEM((SUPER, SUPER), BF),
            pltpu.VMEM((8, CH, SUPER), BF),
            pltpu.VMEM((SUPER, SUPER), BF),
            dma((3,)),
            dma((2, 4)), dma((2, 4)),
            dma((2, 4)), dma((2,)),
            dma((18,)), dma((18,)),
            dma((NSUB, 6)), dma((NSUB, 6)),
            dma((8,)), dma((8,)),
            dma((2, 8)), dma((2, 8)),
        ],
        compiler_params=pltpu.CompilerParams(
            collective_id=0, has_side_effects=True, vmem_limit_bytes=60 << 20
        ),
        cost_estimate=pl.CostEstimate(flops=2 * 2048 * 2048 * 2048, bytes_accessed=8 << 20, transcendentals=0),
        name="selected_inverse",
    )(inverse_anc, factor_panel, pattern, diag_inverse)


def solution(mesh):
    return jax.shard_map(
        local,
        mesh=mesh,
        in_specs=(P("row", "col"), P("row", "col"), P(), P("col", None, None)),
        out_specs=(P("col", "row"), P("col", None, None)),
        check_vma=False,
    )
```

```python
import functools

import jax
import jax.numpy as jnp
from jax import lax
from jax.experimental import pallas as pl
from jax.experimental.pallas import tpu as pltpu
from jax.sharding import PartitionSpec as P

SUPER = 256
ROWS = 2048
HALF = 1024
GROUPS = 4
CH = 16
SUB = 4 * CH
NSUB = 8 * GROUPS
TILE = 256
BF = jnp.bfloat16
F32 = jnp.float32
MESH = pl.DeviceIdType.MESH

MEMBERS = {
    "own": ((0, 0),),
    "near": ((1, 0), (2, 0), (0, 1)),
    "two": ((3, 0),),
    "far": ((1, 1), (2, 1), (3, 1)),
}
LAYOUT = [
    ("own", 0), ("own", 1), ("own", 2), ("own", 3), ("near", 0), ("near", 1), ("near", 2), ("two", 0),
    ("far", 0), ("near", 3), ("two", 1), ("far", 1), ("two", 2), ("far", 2), ("two", 3), ("far", 3),
]
SHARDS = []
BASE = {}
for what, group in LAYOUT:
    BASE[what, group] = len(SHARDS)
    SHARDS += [(kind, fam, group) for kind, fam in MEMBERS[what]]
ZOFF = {0: 0, 1: 3, 2: 1, 3: 2}

UNITS = [(0, 1), (1, 1), (2, 1), (3, 1), (4, 3), (7, 3), (10, 4), (14, 3), (17, 4), (21, 4), (25, 4), (29, 1), (30, 1), (31, 1)]


def schedule():
    yield "over_x", 0
    yield "over_x", 1
    yield "over_x", 2
    yield "own", 0
    yield "over_x", 3
    yield "swap", 0
    yield "mul", (0, 1)
    yield "r1", 0
    for g in (1, 2, 3):
        yield "own", g
        yield "mul", (g, 1)
        yield "r1", g
        yield "r2", g - 1
    waits = {
        4: [("near", 0)], 5: [("near", 1)], 6: [("near", 2), ("two", 0)], 7: [("far", 0)],
        8: [("near", 3), ("two", 1)], 9: [("far", 1), ("two", 2)], 10: [("far", 2), ("two", 3)],
    }
    for u in range(4, 11):
        yield from waits[u]
        yield "mul", UNITS[u]
        yield "r1", u
        yield "r2", u - 1
        if u == 4:
            yield "r3", 0
            yield "r3", 1
        yield "r3", u - 2
        if u >= 8:
            yield "fin", u - 4
    yield "r2", 10
    yield "r3", 9
    yield "far", 3
    yield "mul", (29, 3)
    for u in (11, 12, 13):
        yield "r1", u
    yield "r3", 10
    for u in (11, 12, 13):
        yield "r2", u
    for u in (7, 8):
        yield "fin", u
    yield "fin", 9
    yield "r3", 11
    yield "fin", 10
    yield "r3", 12
    yield "r3", 13
    yield "send_early", 0
    for u in (11, 12, 13):
        yield "fin", u
    yield "sum_early", 0


def kernel(
    a_ref, f_hbm, pat_ref, dinv_hbm,
    u_hbm, diag_hbm,
    f_ref, dinv_ref, u_ref, diag_ref, afull, mt, mask, tz, m, p, pown, ra, rb, da, db, ea, eb, s2, ysend, yrecv, early, early_in, early_sum, late, corr,
    io_sem, u_sem, a_sem, tz_s, tz_r, tx_s, tx_r, m_s, m_r, rs_s, rs_r, y_s, y_r, d_s, d_r,
):
    row = lax.axis_index("row")
    col = lax.axis_index("col")
    z, yl = row // 2, row % 2
    x, yh, h = col // 4, (col // 2) % 2, col % 2

    def dev(z=z, yl=yl, x=x, yh=yh, h=h):
        return (z * 2 + yl, (x * 2 + yh) * 2 + h)

    def remote(src, dst, ssem, rsem, to):
        return pltpu.make_async_remote_copy(
            src_ref=src, dst_ref=dst, send_sem=ssem, recv_sem=rsem, device_id=to, device_id_type=MESH
        )

    def arrive(ref, sem):
        pltpu.make_async_copy(ref, ref, sem).wait()

    sends = []
    stores = []

    def send(src, dst, ssem, rsem, to):
        copy = remote(src, dst, ssem, rsem, to)
        copy.start()
        sends.append(copy)

    zp, zm = (z + 1) % 4, (z + 3) % 4
    xp, xm = (x + 1) % 4, (x + 3) % 4

    f_copy = pltpu.make_async_copy(f_hbm, f_ref, io_sem.at[0])
    f_copy.start()

    barrier = pltpu.get_barrier_semaphore()
    partners = [dev(h=1 - h), dev(yh=1 - yh)]
    for dz in range(4):
        for fl in range(2):
            if dz or fl:
                partners.append(dev(z=(z + dz) % 4, yl=(yl + fl) % 2))
    for dx in range(4):
        for fl in range(2):
            if dx or fl:
                partners.append(dev(x=(x + dx) % 4, yl=(yl + fl) % 2, yh=(yh + fl) % 2))
    for to in partners:
        pl.semaphore_signal(barrier, inc=1, device_id=to, device_id_type=MESH)

    a_local = pltpu.make_async_copy(a_ref, afull.at[h], a_sem.at[0])
    dinv_copy = pltpu.make_async_copy(dinv_hbm, dinv_ref, io_sem.at[1])
    f_copy.wait()
    a_local.start()
    dinv_copy.start()

    for b in range(8):
        keep = pat_ref[col, row * 8 + b].astype(F32)
        mask[:, b * 256:(b + 1) * 256] = jnp.full((8, 256), keep, F32)
        block = f_ref[b * 256:(b + 1) * 256, :].astype(F32)
        mt[:, b * 256:(b + 1) * 256] = (block.T * keep).astype(BF)

    pl.semaphore_wait(barrier, len(partners))

    def piece(zz, g):
        return mt.at[pl.ds(pl.multiple_of(zz * 64 + g * CH, CH), CH)]

    for g in range(GROUPS):
        for dz in (1, 3, 2) if g % 2 == 0 else (1, 3, 2, 0):
            zz = (z + dz) % 4
            k = (4 - dz) % 4
            to = dev(z=zz) if g % 2 == 0 else dev(z=zz, yl=1 - yl)
            send(piece(zz, g), tz.at[g, k], tz_s.at[g, k], tz_r.at[g, k], to)
    send(a_ref, afull.at[h], a_sem.at[1], a_sem.at[2], dev(h=1 - h))

    tx_waits = []
    def over_x(g):
        nyh, nyl = (yl, yh) if g % 2 == 0 else (1 - yl, 1 - yh)
        same_y = yl == yh if g % 2 == 0 else yl != yh
        for k in (0, 1, 3, 2):
            if g % 2 == 0 and k == 0:
                src = piece(z, g)
            else:
                src = tz.at[g, k]
                arrive(src, tz_r.at[g, k])
            xd = (z + k) % 4
            slot = (x + 4 - xd) % 4
            dst = m.at[pl.ds(pl.multiple_of(g * SUB + slot * CH, CH), CH)]
            remote_copy = remote(src, dst, tx_s.at[g, k], tx_r.at[g], dev(x=xd, yh=nyh, yl=nyl))
            local_copy = pltpu.make_async_copy(src, dst, tx_r.at[g])
            here = jnp.logical_and(same_y, xd == x)

            @pl.when(here)
            def _():
                local_copy.start()

            @pl.when(jnp.logical_not(here))
            def _():
                remote_copy.start()

            tx_waits.append((here, remote_copy))

    def msub(s, lo=0, n=SUB):
        return m.at[s * SUB + lo:s * SUB + lo + n]

    def multiply(s0, n):
        rows = slice(s0 * SUB, (s0 + n) * SUB)

        def tile(it, carry):
            at = pl.ds(pl.multiple_of(it * TILE, TILE), TILE)
            dims = (((1,), (1,)), ((), ()))
            acc = lax.dot_general(m[rows, :HALF], afull[0, at, :], dims, preferred_element_type=F32)
            acc += lax.dot_general(m[rows, HALF:], afull[1, at, :], dims, preferred_element_type=F32)
            for i in range(n):
                at_row = slice((s0 + i) * CH, (s0 + i + 1) * CH)
                pown[at_row, at] = acc[i * SUB:i * SUB + CH]
                for k in range(3):
                    lo = i * SUB + (k + 1) * CH
                    p[k, at_row, at] = acc[lo:lo + CH].astype(BF)
            return carry

        lax.fori_loop(0, ROWS // TILE, tile, 0)

    half = (slice(0, HALF), slice(HALF, ROWS))

    def rows_of(b):
        s0, n = UNITS[b]
        return slice(s0 * CH, (s0 + n) * CH)

    def x_send(b, i, src, dst, to):
        send(src, dst, rs_s.at[b, i], rs_r.at[b, i], to)

    def reduce_1(b):
        r = rows_of(b)
        x_send(b, 0, p.at[1, r, half[0]], ra.at[r], dev(x=xp))
        x_send(b, 1, p.at[1, r, half[1]], rb.at[r], dev(x=xm))
        x_send(b, 2, p.at[0, r, half[1]], db.at[r], dev(x=xp))
        x_send(b, 3, p.at[2, r, half[0]], da.at[r], dev(x=xm))

    def reduce_2(b):
        r = rows_of(b)
        arrive(ra.at[r], rs_r.at[b, 0])
        p[0, r, half[0]] = (p[0, r, half[0]].astype(F32) + ra[r].astype(F32)).astype(BF)
        x_send(b, 4, p.at[0, r, half[0]], ea.at[r], dev(x=xp))
        arrive(rb.at[r], rs_r.at[b, 1])
        p[2, r, half[1]] = (p[2, r, half[1]].astype(F32) + rb[r].astype(F32)).astype(BF)
        x_send(b, 5, p.at[2, r, half[1]], eb.at[r], dev(x=xm))

    def mine(g):
        return (yl + g + yh) % 2

    def reduce_3(b):
        r = rows_of(b)
        arrive(db.at[r], rs_r.at[b, 2])
        arrive(da.at[r], rs_r.at[b, 3])
        arrive(ea.at[r], rs_r.at[b, 4])
        arrive(eb.at[r], rs_r.at[b, 5])
        s0, n = UNITS[b]
        pairs = []
        for s in range(s0, s0 + n):
            kind, fam, g = SHARDS[s]
            pair = kind * GROUPS + g
            r = slice(s * CH, (s + 1) * CH)
            s2[pair, fam, :, half[0]] = pown[r, half[0]] + (ea[r].astype(F32) + da[r].astype(F32))
            s2[pair, fam, :, half[1]] = pown[r, half[1]] + (eb[r].astype(F32) + db[r].astype(F32))
            if fam == 1:
                ysend[pair] = s2[pair, 1 - mine(g)].astype(BF)
                send(ysend.at[pair], yrecv.at[pair], y_s.at[pair], y_r.at[pair], dev(yh=1 - yh))
                pairs.append(pair)
        return pairs

    def finish(pair):
        kind, g = pair // GROUPS, pair % GROUPS
        arrive(yrecv.at[pair], y_r.at[pair])
        total = s2[pair, mine(g)] + yrecv[pair].astype(F32)
        zz = (z + ZOFF[kind]) % 4
        at = pl.ds(pl.multiple_of(zz * 64 + g * CH, CH), CH)
        u_ref[at, :] = (-total * mask[0:1, :]).astype(BF)
        copy = pltpu.make_async_copy(u_ref.at[at], u_hbm.at[at], u_sem.at[pair])
        copy.start()
        stores.append(copy)

    def m_send(s, to, at, sem=None, lo=0, n=SUB):
        sem = at if sem is None else sem
        send(msub(s, lo, n), msub(at, lo, n), m_s.at[sem], m_r.at[sem], to)

    def arrival(what, g):
        s = BASE[what, g]
        if what == "own":
            to = BASE["near", g]
            arrive(msub(s), tx_r.at[g])
            m_send(s, dev(z=zp), to)
            m_send(s, dev(z=zm), to + 1)
            m_send(s, dev(yl=1 - yl), to + 2)
        elif what == "near":
            two, to = BASE["two", g], BASE["far", g]
            for i in range(3):
                arrive(msub(s + i), m_r.at[s + i])
            m_send(s, dev(z=zp), two, two, 0, SUB // 2)
            m_send(s + 1, dev(z=zm), two, NSUB + g, SUB // 2, SUB // 2)
            m_send(s + 2, dev(z=zp), to)
            m_send(s + 2, dev(z=zm), to + 1)
        elif what == "two":
            arrive(msub(s, 0, SUB // 2), m_r.at[s])
            arrive(msub(s, SUB // 2, SUB // 2), m_r.at[NSUB + g])
            m_send(s, dev(yl=1 - yl), BASE["far", g] + 2)
        else:
            for i in range(3):
                arrive(msub(s + i), m_r.at[s + i])

    def others():
        for k in range(1, 8):
            r = (row + k) % 8
            yield k, r, (r, col)

    def correction(lo, n):
        return lax.dot_general(u_ref[lo:lo + n], mt[...], (((1,), (1,)), ((), ())), preferred_element_type=F32)

    def share(r):
        return pl.ds(pl.multiple_of(r * 24, 8), 24)

    def send_early():
        for zz in range(4):
            early[zz * 48:(zz + 1) * 48] = correction(zz * 64, 48)
        for k, r, to in others():
            send(early.at[share(r)], early_in.at[8 - k], d_s.at[0, k], d_r.at[0, 8 - k], to)

    def sum_early():
        total = early[share(row), :]
        for k in range(1, 8):
            arrive(early_in.at[k], d_r.at[0, k])
            total += early_in[k]
        early_in[0] = total
        for k, r, to in others():
            send(early_in.at[0], early_sum.at[row], d_s.at[1, k], d_r.at[1, 8 - k], to)
        early_sum[row] = total

    def arrive_early():
        for k, r, to in others():
            arrive(early_sum.at[r], d_r.at[1, k])
        for zz in range(4):
            for i in range(2):
                lo = zz * 64 + i * 24
                corr[lo:lo + 24] = early_sum[zz * 2 + i]

    ready = {}
    for what, arg in schedule():
        if what == "over_x":
            over_x(arg)
        elif what == "swap":
            a_local.wait()
            arrive(afull.at[1 - h], a_sem.at[2])
        elif what == "mul":
            multiply(*arg)
        elif what == "r1":
            reduce_1(arg)
        elif what == "r2":
            reduce_2(arg)
        elif what == "r3":
            ready[arg] = reduce_3(arg)
        elif what == "send_early":
            send_early()
        elif what == "sum_early":
            sum_early()
        elif what == "fin":
            for pair in ready[arg]:
                finish(pair)
        else:
            arrival(what, arg)

    for zz in range(4):
        late[row, zz * CH:(zz + 1) * CH] = correction(zz * 64 + 48, CH).astype(BF)
    for k, r, to in others():
        send(late.at[row], late.at[row], d_s.at[2, k], d_r.at[2, 8 - k], to)
    arrive_early()
    for k, r, to in others():
        arrive(late.at[r], d_r.at[2, k])
    total = late[0].astype(F32)
    for r in range(1, 8):
        total += late[r].astype(F32)
    for zz in range(4):
        corr[zz * 64 + 48:(zz + 1) * 64] = total[zz * CH:(zz + 1) * CH]
    dinv_copy.wait()
    diag_ref[0] = dinv_ref[0] - corr[...].T
    copy = pltpu.make_async_copy(diag_ref, diag_hbm, io_sem.at[2])
    copy.start()
    stores.append(copy)

    for copy in stores:
        copy.wait()
    for copy in sends:
        copy.wait_send()
    for here, remote_copy in tx_waits:
        @pl.when(jnp.logical_not(here))
        def _():
            remote_copy.wait_send()


def place(u_in, diag_in, u_out, diag_out):
    u_out[...] = u_in[...]
    diag_out[...] = diag_in[...]


def local(inverse_anc, factor_panel, pattern, diag_inverse):
    hbm = pl.BlockSpec(memory_space=pl.ANY)
    dma = pltpu.SemaphoreType.DMA
    blocks = [pl.BlockSpec((64, ROWS), lambda i: (i, 0)), pl.BlockSpec((1, 64, SUPER), lambda i: (0, i, 0))]
    part = pltpu.VMEM((NSUB * CH, HALF), BF)
    out = pl.pallas_call(
        kernel,
        out_shape=(
            jax.ShapeDtypeStruct((SUPER, ROWS), BF),
            jax.ShapeDtypeStruct((1, SUPER, SUPER), F32),
        ),
        in_specs=[hbm, hbm, pl.BlockSpec(memory_space=pltpu.SMEM), hbm],
        out_specs=(hbm, hbm),
        scratch_shapes=[
            pltpu.VMEM((ROWS, SUPER), BF),
            pltpu.VMEM((1, SUPER, SUPER), F32),
            pltpu.VMEM((SUPER, ROWS), BF),
            pltpu.VMEM((1, SUPER, SUPER), F32),
            pltpu.VMEM((2, ROWS, HALF), BF),
            pltpu.VMEM((SUPER, ROWS), BF),
            pltpu.VMEM((8, ROWS), F32),
            pltpu.VMEM((GROUPS, 4, CH, ROWS), BF),
            pltpu.VMEM((NSUB * SUB, ROWS), BF),
            pltpu.VMEM((3, NSUB * CH, ROWS), BF),
            pltpu.VMEM((NSUB * CH, ROWS), F32),
            part, part, part, part, part, part,
            pltpu.VMEM((4 * GROUPS, 2, CH, ROWS), F32),
            pltpu.VMEM((4 * GROUPS, CH, ROWS), BF),
            pltpu.VMEM((4 * GROUPS, CH, ROWS), BF),
            pltpu.VMEM((192, SUPER), F32),
            pltpu.VMEM((8, 24, SUPER), F32),
            pltpu.VMEM((8, 24, SUPER), F32),
            pltpu.VMEM((8, 64, SUPER), BF),
            pltpu.VMEM((SUPER, SUPER), F32),
            dma((3,)), dma((4 * GROUPS,)),
            dma((3,)),
            dma((GROUPS, 4)), dma((GROUPS, 4)),
            dma((GROUPS, 4)), dma((GROUPS,)),
            dma((NSUB + GROUPS,)), dma((NSUB + GROUPS,)),
            dma((len(UNITS), 6)), dma((len(UNITS), 6)),
            dma((4 * GROUPS,)), dma((4 * GROUPS,)),
            dma((3, 8)), dma((3, 8)),
        ],
        compiler_params=pltpu.CompilerParams(
            collective_id=0, has_side_effects=True, vmem_limit_bytes=60 << 20
        ),
        cost_estimate=pl.CostEstimate(flops=2 * 2048 * 2048 * 2048, bytes_accessed=8 << 20, transcendentals=0),
        name="selected_inverse",
    )(inverse_anc, factor_panel, pattern, diag_inverse)
    return pl.pallas_call(
        place,
        out_shape=tuple(jax.ShapeDtypeStruct(o.shape, o.dtype) for o in out),
        grid=(4,),
        in_specs=blocks,
        out_specs=tuple(blocks),
        name="place_outputs",
    )(*out)


def solution(mesh):
    return jax.shard_map(
        local,
        mesh=mesh,
        in_specs=(P("row", "col"), P("row", "col"), P(), P("col", None, None)),
        out_specs=(P("col", "row"), P("col", None, None)),
        check_vma=False,
    )
```

```python
import functools

import jax
import jax.numpy as jnp
from jax import lax
from jax.experimental import pallas as pl
from jax.experimental.pallas import tpu as pltpu
from jax.sharding import PartitionSpec as P

SUPER = 256
ROWS = 2048
HALF = 1024
GROUPS = 4
CH = 16
SUB = 4 * CH
NSUB = 8 * GROUPS
TILE = 1024
BF = jnp.bfloat16
F32 = jnp.float32
MESH = pl.DeviceIdType.MESH

MEMBERS = {
    "own": ((0, 0),),
    "near": ((1, 0), (2, 0), (0, 1)),
    "two": ((3, 0),),
    "far": ((1, 1), (2, 1), (3, 1)),
}
LAYOUT = [
    ("own", 0), ("own", 1), ("own", 2), ("own", 3), ("near", 0), ("near", 1), ("near", 2), ("two", 0),
    ("far", 0), ("near", 3), ("two", 1), ("far", 1), ("two", 2), ("far", 2), ("two", 3), ("far", 3),
]
SHARDS = []
BASE = {}
for what, group in LAYOUT:
    BASE[what, group] = len(SHARDS)
    SHARDS += [(kind, fam, group) for kind, fam in MEMBERS[what]]
ZOFF = {0: 0, 1: 3, 2: 1, 3: 2}

PATH = "abcb"
FLIP = [int(path == "c") for path in PATH]

UNITS = [(0, 1), (1, 1), (2, 1), (3, 1), (4, 3), (7, 3), (10, 4), (14, 3), (17, 4), (21, 4), (25, 4), (29, 1), (30, 1), (31, 1)]


def schedule():
    yield "over_x", 0
    yield "over_x", 2
    yield "over_x", 1
    yield "own", 0
    yield "over_x", 3
    yield "swap", 0
    yield "mul", (0, 1)
    yield "r1", 0
    yield "own", 2
    yield "own", 1
    yield "mul", (1, 2)
    yield "r1", 1
    yield "r1", 2
    yield "r2", 0
    yield "own", 3
    yield "r2", 1
    yield "r2", 2
    yield "r3", 0
    yield "near", 0
    yield "mul", (3, 4)
    yield "r1", 3
    yield "r1", 4
    yield "r3", 1
    yield "r2", 3
    yield "near", 1
    yield "mul", UNITS[5]
    yield "r1", 5
    yield "near", 2
    yield "r2", 4
    yield "r3", 2
    yield "two", 0
    yield "mul", UNITS[6]
    yield "r1", 6
    yield "r2", 5
    yield "r3", 3
    yield "near", 3
    yield "far", 0
    yield "mul", UNITS[7]
    yield "r1", 7
    yield "two", 1
    yield "r2", 6
    yield "r3", 4
    yield "mul", UNITS[8]
    yield "r1", 8
    yield "two", 2
    yield "r2", 7
    yield "r3", 5
    yield "fin", 4
    yield "far", 1
    yield "mul", UNITS[9]
    yield "r1", 9
    yield "two", 3
    yield "r2", 8
    yield "r3", 6
    yield "fin", 5
    yield "far", 2
    yield "mul", UNITS[10]
    yield "r1", 10
    yield "r2", 9
    yield "r3", 7
    yield "fin", 6
    yield "r3", 8
    yield "r2", 10
    yield "r3", 9
    yield "far", 3
    yield "mul", (29, 3)
    for u in (11, 12, 13):
        yield "r1", u
    yield "r3", 10
    for u in (11, 12, 13):
        yield "r2", u
    for u in (7, 8, 9, 10):
        yield "fin", u
    yield "send_early", 0
    for u in (11, 12, 13):
        yield "r3", u
    yield "sum_early", 0
    for u in (11, 12, 13):
        yield "fin", u


def kernel(
    a_ref, f_hbm, pat_ref, dinv_hbm,
    u_hbm, diag_hbm,
    f_ref, dinv_ref, u_ref, diag_ref, afull, mt, mask, tz, m, p, pown, ra, rb, da, db, ea, eb, s2, ysend, yrecv, early, early_in, early_sum, late, corr,
    io_sem, u_sem, a_sem, tz_s, tz_r, tx_s, tx_r, m_s, m_r, rs_s, rs_r, y_s, y_r, d_s, d_r,
):
    row = lax.axis_index("row")
    col = lax.axis_index("col")
    z, yl = row // 2, row % 2
    x, yh, h = col // 4, (col // 2) % 2, col % 2

    def dev(z=z, yl=yl, x=x, yh=yh, h=h):
        return (z * 2 + yl, (x * 2 + yh) * 2 + h)

    def remote(src, dst, ssem, rsem, to):
        return pltpu.make_async_remote_copy(
            src_ref=src, dst_ref=dst, send_sem=ssem, recv_sem=rsem, device_id=to, device_id_type=MESH
        )

    def arrive(ref, sem):
        pltpu.make_async_copy(ref, ref, sem).wait()

    sends = []
    stores = []

    def send(src, dst, ssem, rsem, to):
        copy = remote(src, dst, ssem, rsem, to)
        copy.start()
        sends.append(copy)

    zp, zm = (z + 1) % 4, (z + 3) % 4
    xp, xm = (x + 1) % 4, (x + 3) % 4

    f_copy = pltpu.make_async_copy(f_hbm, f_ref, io_sem.at[0])
    f_copy.start()

    barrier = pltpu.get_barrier_semaphore()
    partners = [dev(h=1 - h), dev(yh=1 - yh)]
    for dz in range(4):
        for fl in range(2):
            if dz or fl:
                partners.append(dev(z=(z + dz) % 4, yl=(yl + fl) % 2))
    for dx in range(4):
        for fl in range(2):
            if dx or fl:
                partners.append(dev(x=(x + dx) % 4, yl=(yl + fl) % 2, yh=(yh + fl) % 2))
    for dz in range(1, 4):
        partners.append(dev(z=(z + dz) % 4, yl=1 - yl, yh=1 - yh))
    for to in partners:
        pl.semaphore_signal(barrier, inc=1, device_id=to, device_id_type=MESH)

    a_local = pltpu.make_async_copy(a_ref, afull.at[h], a_sem.at[0])
    dinv_copy = pltpu.make_async_copy(dinv_hbm, dinv_ref, io_sem.at[1])
    f_copy.wait()
    a_local.start()
    dinv_copy.start()

    for b in range(8):
        keep = pat_ref[col, row * 8 + b].astype(F32)
        mask[:, b * 256:(b + 1) * 256] = jnp.full((8, 256), keep, F32)
        block = f_ref[b * 256:(b + 1) * 256, :].astype(F32)
        mt[:, b * 256:(b + 1) * 256] = (block.T * keep).astype(BF)

    pl.semaphore_wait(barrier, len(partners))

    def piece(zz, g):
        return mt.at[pl.ds(pl.multiple_of(zz * 64 + g * CH, CH), CH)]

    tx_waits = []

    def send_unless(here, src, dst, ssem, rsem, to):
        remote_copy = remote(src, dst, ssem, rsem, to)
        local_copy = pltpu.make_async_copy(src, dst, rsem)

        @pl.when(here)
        def _():
            local_copy.start()

        @pl.when(jnp.logical_not(here))
        def _():
            remote_copy.start()

        tx_waits.append((here, remote_copy))

    for g in (0, 2, 1, 3):
        for dz in (1, 3, 2, 0):
            zz = (z + dz) % 4
            k = (4 - dz) % 4
            args = piece(zz, g), tz.at[g, k], tz_s.at[g, k], tz_r.at[g, k]
            if PATH[g] == "a" and dz == 0:
                send_unless(yl == yh, *args, dev(yh=yl, yl=yh))
            elif PATH[g] == "a":
                send(*args, dev(z=zz, yh=yl, yl=yh))
            elif PATH[g] == "c":
                send(*args, dev(z=zz, yl=1 - yl))
            elif dz != 0:
                send(*args, dev(z=zz))
    send(a_ref, afull.at[h], a_sem.at[1], a_sem.at[2], dev(h=1 - h))

    def over_x(g):
        path = PATH[g]
        nyh, nyl = {"a": (yh, yl), "b": (yl, yh), "c": (1 - yl, 1 - yh)}[path]
        same_y = {"a": True, "b": yl == yh, "c": yl != yh}[path]
        for k in (0, 1, 3, 2):
            if path == "b" and k == 0:
                src = piece(z, g)
            else:
                src = tz.at[g, k]
                arrive(src, tz_r.at[g, k])
            xd = (z + k) % 4
            slot = (x + 4 - xd) % 4
            dst = m.at[pl.ds(pl.multiple_of(g * SUB + slot * CH, CH), CH)]
            here = jnp.logical_and(same_y, xd == x)
            send_unless(here, src, dst, tx_s.at[g, k], tx_r.at[g], dev(x=xd, yh=nyh, yl=nyl))

    def msub(s, lo=0, n=SUB):
        return m.at[s * SUB + lo:s * SUB + lo + n]

    def multiply(s0, n):
        rows = slice(s0 * SUB, (s0 + n) * SUB)

        for hf in range(2):

            def tile(it, carry):
                col_at = pl.ds(pl.multiple_of(it * TILE, TILE), TILE)
                at = pl.ds(pl.multiple_of(hf * HALF + it * TILE, TILE), TILE)
                dims = (((1,), (1,)), ((), ()))
                acc = lax.dot_general(m[rows, :HALF], afull[0, at, :], dims, preferred_element_type=F32)
                acc += lax.dot_general(m[rows, HALF:], afull[1, at, :], dims, preferred_element_type=F32)
                for i in range(n):
                    at_row = slice((s0 + i) * CH, (s0 + i + 1) * CH)
                    pown[at_row, at] = acc[i * SUB:i * SUB + CH]
                    for k in range(3):
                        lo = i * SUB + (k + 1) * CH
                        p[k, hf, at_row, col_at] = acc[lo:lo + CH].astype(BF)
                return carry

            lax.fori_loop(0, HALF // TILE, tile, 0)

    half = (slice(0, HALF), slice(HALF, ROWS))

    def rows_of(b):
        s0, n = UNITS[b]
        return slice(s0 * CH, (s0 + n) * CH)

    def x_send(b, i, src, dst, to):
        send(src, dst, rs_s.at[b, i], rs_r.at[b, i], to)

    def reduce_1(b):
        r = rows_of(b)
        x_send(b, 0, p.at[1, 0, r], ra.at[r], dev(x=xp))
        x_send(b, 1, p.at[1, 1, r], rb.at[r], dev(x=xm))
        x_send(b, 2, p.at[0, 1, r], db.at[r], dev(x=xp))
        x_send(b, 3, p.at[2, 0, r], da.at[r], dev(x=xm))

    def reduce_2(b):
        r = rows_of(b)
        arrive(ra.at[r], rs_r.at[b, 0])
        p[0, 0, r] = (p[0, 0, r].astype(F32) + ra[r].astype(F32)).astype(BF)
        x_send(b, 4, p.at[0, 0, r], ea.at[r], dev(x=xp))
        arrive(rb.at[r], rs_r.at[b, 1])
        p[2, 1, r] = (p[2, 1, r].astype(F32) + rb[r].astype(F32)).astype(BF)
        x_send(b, 5, p.at[2, 1, r], eb.at[r], dev(x=xm))

    def mine(g):
        return (yl + FLIP[g] + yh) % 2

    def reduce_3(b):
        r = rows_of(b)
        arrive(db.at[r], rs_r.at[b, 2])
        arrive(da.at[r], rs_r.at[b, 3])
        arrive(ea.at[r], rs_r.at[b, 4])
        arrive(eb.at[r], rs_r.at[b, 5])
        s0, n = UNITS[b]
        pairs = []
        for s in range(s0, s0 + n):
            kind, fam, g = SHARDS[s]
            pair = kind * GROUPS + g
            r = slice(s * CH, (s + 1) * CH)
            s2[pair, fam, :, half[0]] = pown[r, half[0]] + (ea[r].astype(F32) + da[r].astype(F32))
            s2[pair, fam, :, half[1]] = pown[r, half[1]] + (eb[r].astype(F32) + db[r].astype(F32))
            if fam == 1:
                ysend[pair] = s2[pair, 1 - mine(g)].astype(BF)
                send(ysend.at[pair], yrecv.at[pair], y_s.at[pair], y_r.at[pair], dev(yh=1 - yh))
                pairs.append(pair)
        return pairs

    def finish(pair):
        kind, g = pair // GROUPS, pair % GROUPS
        arrive(yrecv.at[pair], y_r.at[pair])
        total = s2[pair, mine(g)] + yrecv[pair].astype(F32)
        zz = (z + ZOFF[kind]) % 4
        at = pl.ds(pl.multiple_of(zz * 64 + g * CH, CH), CH)
        u_ref[at, :] = (-total * mask[0:1, :]).astype(BF)
        copy = pltpu.make_async_copy(u_ref.at[at], u_hbm.at[at], u_sem.at[pair])
        copy.start()
        stores.append(copy)

    def m_send(s, to, at, sem=None, lo=0, n=SUB):
        sem = at if sem is None else sem
        send(msub(s, lo, n), msub(at, lo, n), m_s.at[sem], m_r.at[sem], to)

    def arrival(what, g):
        s = BASE[what, g]
        if what == "own":
            to = BASE["near", g]
            arrive(msub(s), tx_r.at[g])
            m_send(s, dev(z=zp), to)
            m_send(s, dev(z=zm), to + 1)
            m_send(s, dev(yl=1 - yl), to + 2)
        elif what == "near":
            two, to = BASE["two", g], BASE["far", g]
            for i in range(3):
                arrive(msub(s + i), m_r.at[s + i])
            m_send(s, dev(z=zp), two, two, 0, SUB // 2)
            m_send(s + 1, dev(z=zm), two, NSUB + g, SUB // 2, SUB // 2)
            m_send(s + 2, dev(z=zp), to)
            m_send(s + 2, dev(z=zm), to + 1)
        elif what == "two":
            arrive(msub(s, 0, SUB // 2), m_r.at[s])
            arrive(msub(s, SUB // 2, SUB // 2), m_r.at[NSUB + g])
            m_send(s, dev(yl=1 - yl), BASE["far", g] + 2)
        else:
            for i in range(3):
                arrive(msub(s + i), m_r.at[s + i])

    def others():
        for k in range(1, 8):
            r = (row + k) % 8
            yield k, r, (r, col)

    def correction(parts):
        rows = jnp.concatenate([u_ref[lo:lo + n] for lo, n in parts], axis=0)
        return lax.dot_general(rows, mt[...], (((1,), (1,)), ((), ())), preferred_element_type=F32)

    def share(r):
        return pl.ds(pl.multiple_of(r * 24, 8), 24)

    def send_early():
        early[...] = correction([(zz * 64, 48) for zz in range(4)])
        for k, r, to in others():
            send(early.at[share(r)], early_in.at[8 - k], d_s.at[0, k], d_r.at[0, 8 - k], to)

    def sum_early():
        total = early[share(row), :]
        for k in range(1, 8):
            arrive(early_in.at[k], d_r.at[0, k])
            total += early_in[k]
        early_in[0] = total
        for k, r, to in others():
            send(early_in.at[0], early_sum.at[row], d_s.at[1, k], d_r.at[1, 8 - k], to)
        early_sum[row] = total

    def arrive_early():
        for k, r, to in others():
            arrive(early_sum.at[r], d_r.at[1, k])
        for zz in range(4):
            for i in range(2):
                lo = zz * 64 + i * 24
                corr[lo:lo + 24] = early_sum[zz * 2 + i]

    ready = {}
    for what, arg in schedule():
        if what == "over_x":
            over_x(arg)
        elif what == "swap":
            a_local.wait()
            arrive(afull.at[1 - h], a_sem.at[2])
        elif what == "mul":
            multiply(*arg)
        elif what == "r1":
            reduce_1(arg)
        elif what == "r2":
            reduce_2(arg)
        elif what == "r3":
            ready[arg] = reduce_3(arg)
        elif what == "send_early":
            send_early()
        elif what == "sum_early":
            sum_early()
        elif what == "fin":
            for pair in ready[arg]:
                finish(pair)
        else:
            arrival(what, arg)

    late[row] = correction([(zz * 64 + 48, CH) for zz in range(4)]).astype(BF)
    for k, r, to in others():
        send(late.at[row], late.at[row], d_s.at[2, k], d_r.at[2, 8 - k], to)
    arrive_early()
    for k, r, to in others():
        arrive(late.at[r], d_r.at[2, k])
    total = late[0].astype(F32)
    for r in range(1, 8):
        total += late[r].astype(F32)
    for zz in range(4):
        corr[zz * 64 + 48:(zz + 1) * 64] = total[zz * CH:(zz + 1) * CH]
    dinv_copy.wait()
    diag_ref[0] = dinv_ref[0] - corr[...].T
    copy = pltpu.make_async_copy(diag_ref, diag_hbm, io_sem.at[2])
    copy.start()
    stores.append(copy)

    for copy in stores:
        copy.wait()
    for copy in sends:
        copy.wait_send()
    for here, remote_copy in tx_waits:
        @pl.when(jnp.logical_not(here))
        def _():
            remote_copy.wait_send()


def place(u_in, diag_in, u_out, diag_out):
    u_out[...] = u_in[...]
    diag_out[...] = diag_in[...]


def local(inverse_anc, factor_panel, pattern, diag_inverse):
    hbm = pl.BlockSpec(memory_space=pl.ANY)
    dma = pltpu.SemaphoreType.DMA
    blocks = [pl.BlockSpec((128, ROWS), lambda i: (i, 0)), pl.BlockSpec((1, 128, SUPER), lambda i: (0, i, 0))]
    part = pltpu.VMEM((NSUB * CH, HALF), BF)
    out = pl.pallas_call(
        kernel,
        out_shape=(
            jax.ShapeDtypeStruct((SUPER, ROWS), BF),
            jax.ShapeDtypeStruct((1, SUPER, SUPER), F32),
        ),
        in_specs=[hbm, hbm, pl.BlockSpec(memory_space=pltpu.SMEM), hbm],
        out_specs=(hbm, hbm),
        scratch_shapes=[
            pltpu.VMEM((ROWS, SUPER), BF),
            pltpu.VMEM((1, SUPER, SUPER), F32),
            pltpu.VMEM((SUPER, ROWS), BF),
            pltpu.VMEM((1, SUPER, SUPER), F32),
            pltpu.VMEM((2, ROWS, HALF), BF),
            pltpu.VMEM((SUPER, ROWS), BF),
            pltpu.VMEM((8, ROWS), F32),
            pltpu.VMEM((GROUPS, 4, CH, ROWS), BF),
            pltpu.VMEM((NSUB * SUB, ROWS), BF),
            pltpu.VMEM((3, 2, NSUB * CH, HALF), BF),
            pltpu.VMEM((NSUB * CH, ROWS), F32),
            part, part, part, part, part, part,
            pltpu.VMEM((4 * GROUPS, 2, CH, ROWS), F32),
            pltpu.VMEM((4 * GROUPS, CH, ROWS), BF),
            pltpu.VMEM((4 * GROUPS, CH, ROWS), BF),
            pltpu.VMEM((192, SUPER), F32),
            pltpu.VMEM((8, 24, SUPER), F32),
            pltpu.VMEM((8, 24, SUPER), F32),
            pltpu.VMEM((8, 64, SUPER), BF),
            pltpu.VMEM((SUPER, SUPER), F32),
            dma((3,)), dma((4 * GROUPS,)),
            dma((3,)),
            dma((GROUPS, 4)), dma((GROUPS, 4)),
            dma((GROUPS, 4)), dma((GROUPS,)),
            dma((NSUB + GROUPS,)), dma((NSUB + GROUPS,)),
            dma((len(UNITS), 6)), dma((len(UNITS), 6)),
            dma((4 * GROUPS,)), dma((4 * GROUPS,)),
            dma((3, 8)), dma((3, 8)),
        ],
        compiler_params=pltpu.CompilerParams(
            collective_id=0, has_side_effects=True, vmem_limit_bytes=60 << 20
        ),
        cost_estimate=pl.CostEstimate(flops=2 * 2048 * 2048 * 2048, bytes_accessed=8 << 20, transcendentals=0),
        name="selected_inverse",
    )(inverse_anc, factor_panel, pattern, diag_inverse)
    return pl.pallas_call(
        place,
        out_shape=tuple(jax.ShapeDtypeStruct(o.shape, o.dtype) for o in out),
        grid=(2,),
        in_specs=blocks,
        out_specs=tuple(blocks),
        name="place_outputs",
    )(*out)


def solution(mesh):
    return jax.shard_map(
        local,
        mesh=mesh,
        in_specs=(P("row", "col"), P("row", "col"), P(), P("col", None, None)),
        out_specs=(P("col", "row"), P("col", None, None)),
        check_vma=False,
    )
```

```python
import functools

import jax
import jax.numpy as jnp
from jax import lax
from jax.experimental import pallas as pl
from jax.experimental.pallas import tpu as pltpu
from jax.sharding import PartitionSpec as P

SUPER = 256
ROWS = 2048
HALF = 1024
GROUPS = 4
CH = 16
SUB = 4 * CH
NSUB = 8 * GROUPS
TILE = 1024
BF = jnp.bfloat16
F32 = jnp.float32
MESH = pl.DeviceIdType.MESH

MEMBERS = {
    "own": ((0, 0),),
    "near": ((1, 0), (2, 0), (0, 1)),
    "two": ((3, 0),),
    "far": ((1, 1), (2, 1), (3, 1)),
}
LAYOUT = [
    ("own", 0), ("own", 1), ("own", 2), ("own", 3), ("near", 0), ("near", 1), ("near", 2), ("two", 0),
    ("far", 0), ("near", 3), ("two", 1), ("far", 1), ("two", 2), ("far", 2), ("two", 3), ("far", 3),
]
SHARDS = []
BASE = {}
for what, group in LAYOUT:
    BASE[what, group] = len(SHARDS)
    SHARDS += [(kind, fam, group) for kind, fam in MEMBERS[what]]
ZOFF = {0: 0, 1: 3, 2: 1, 3: 2}

PATH = "abcb"
FLIP = [int(path == "c") for path in PATH]

UNITS = [(0, 1), (1, 1), (2, 1), (3, 1), (4, 3), (7, 3), (10, 4), (14, 3), (17, 4), (21, 4), (25, 4), (29, 1), (30, 1), (31, 1)]


def schedule():
    yield "over_x", 0
    yield "over_x", 2
    yield "over_x", 1
    yield "own", 0
    yield "over_x", 3
    yield "swap", 0
    yield "mul", (0, 1)
    yield "r1", 0
    yield "own", 2
    yield "own", 1
    yield "mul", (1, 2)
    yield "r1", 1
    yield "r1", 2
    yield "r2", 0
    yield "own", 3
    yield "r2", 1
    yield "r2", 2
    yield "r3", 0
    yield "near", 0
    yield "mul", (3, 4)
    yield "r1", 3
    yield "r1", 4
    yield "r3", 1
    yield "r2", 3
    yield "near", 1
    yield "mul", UNITS[5]
    yield "r1", 5
    yield "near", 2
    yield "r2", 4
    yield "r3", 2
    yield "two", 0
    yield "mul", UNITS[6]
    yield "r1", 6
    yield "r2", 5
    yield "r3", 3
    yield "near", 3
    yield "far", 0
    yield "mark", 0
    yield "mul", UNITS[7]
    yield "r1", 7
    yield "two", 1
    yield "r2", 6
    yield "r3", 4
    yield "mul", UNITS[8]
    yield "r1", 8
    yield "two", 2
    yield "r2", 7
    yield "r3", 5
    yield "fin", 4
    yield "far", 1
    yield "mul", UNITS[9]
    yield "r1", 9
    yield "two", 3
    yield "r2", 8
    yield "r3", 6
    yield "fin", 5
    yield "far", 2
    yield "mul", UNITS[10]
    yield "r1", 10
    yield "r2", 9
    yield "r3", 7
    yield "fin", 6
    yield "r3", 8
    yield "drain", 0
    yield "mark", 0
    yield "r2", 10
    yield "r3", 9
    yield "far", 3
    yield "mul", (29, 3)
    for u in (11, 12, 13):
        yield "r1", u
    yield "r3", 10
    for u in (11, 12, 13):
        yield "r2", u
    for u in (7, 8, 9, 10):
        yield "fin", u
    yield "drain", 0
    yield "send_early", 0
    for u in (11, 12, 13):
        yield "r3", u
    yield "sum_early", 0
    for u in (11, 12, 13):
        yield "fin", u


def kernel(
    a_ref, f_hbm, pat_ref, dinv_hbm,
    u_hbm, diag_hbm,
    f_ref, dinv_ref, u_ref, diag_ref, afull, mt, mask, tz, m, p, pown, ra, rb, da, db, ea, eb, s2, ysend, yrecv, early, early_in, early_sum, late, corr,
    io_sem, u_sem, a_sem, tz_s, tz_r, tx_s, tx_r, m_s, m_r, rs_s, rs_r, y_s, y_r, d_s, d_r,
):
    row = lax.axis_index("row")
    col = lax.axis_index("col")
    z, yl = row // 2, row % 2
    x, yh, h = col // 4, (col // 2) % 2, col % 2

    def dev(z=z, yl=yl, x=x, yh=yh, h=h):
        return (z * 2 + yl, (x * 2 + yh) * 2 + h)

    def remote(src, dst, ssem, rsem, to):
        return pltpu.make_async_remote_copy(
            src_ref=src, dst_ref=dst, send_sem=ssem, recv_sem=rsem, device_id=to, device_id_type=MESH
        )

    def arrive(ref, sem):
        pltpu.make_async_copy(ref, ref, sem).wait()

    sends = []
    stores = []

    def send(src, dst, ssem, rsem, to):
        copy = remote(src, dst, ssem, rsem, to)
        copy.start()
        sends.append(copy)

    zp, zm = (z + 1) % 4, (z + 3) % 4
    xp, xm = (x + 1) % 4, (x + 3) % 4

    f_copy = pltpu.make_async_copy(f_hbm, f_ref, io_sem.at[0])
    f_copy.start()

    barrier = pltpu.get_barrier_semaphore()
    partners = [dev(h=1 - h), dev(yh=1 - yh)]
    for dz in range(4):
        for fl in range(2):
            if dz or fl:
                partners.append(dev(z=(z + dz) % 4, yl=(yl + fl) % 2))
    for dx in range(4):
        for fl in range(2):
            if dx or fl:
                partners.append(dev(x=(x + dx) % 4, yl=(yl + fl) % 2, yh=(yh + fl) % 2))
    for dz in range(1, 4):
        partners.append(dev(z=(z + dz) % 4, yl=1 - yl, yh=1 - yh))
    for to in partners:
        pl.semaphore_signal(barrier, inc=1, device_id=to, device_id_type=MESH)

    a_local = pltpu.make_async_copy(a_ref, afull.at[h], a_sem.at[0])
    dinv_copy = pltpu.make_async_copy(dinv_hbm, dinv_ref, io_sem.at[1])
    f_copy.wait()
    a_local.start()
    dinv_copy.start()

    for b in range(8):
        keep = pat_ref[col, row * 8 + b].astype(F32)
        mask[:, b * 256:(b + 1) * 256] = jnp.full((8, 256), keep, F32)
        block = f_ref[b * 256:(b + 1) * 256, :].astype(F32)
        mt[:, b * 256:(b + 1) * 256] = (block.T * keep).astype(BF)

    pl.semaphore_wait(barrier, len(partners))

    def piece(zz, g):
        return mt.at[pl.ds(pl.multiple_of(zz * 64 + g * CH, CH), CH)]

    tx_waits = []

    def send_unless(here, src, dst, ssem, rsem, to):
        remote_copy = remote(src, dst, ssem, rsem, to)
        local_copy = pltpu.make_async_copy(src, dst, rsem)

        @pl.when(here)
        def _():
            local_copy.start()

        @pl.when(jnp.logical_not(here))
        def _():
            remote_copy.start()

        tx_waits.append((here, remote_copy))

    def wait_unless(here, remote_copy):
        @pl.when(jnp.logical_not(here))
        def _():
            remote_copy.wait_send()

    for g in (0, 2, 1, 3):
        for dz in (1, 3, 2, 0):
            zz = (z + dz) % 4
            k = (4 - dz) % 4
            args = piece(zz, g), tz.at[g, k], tz_s.at[g, k], tz_r.at[g, k]
            if PATH[g] == "a" and dz == 0:
                send_unless(yl == yh, *args, dev(yh=yl, yl=yh))
            elif PATH[g] == "a":
                send(*args, dev(z=zz, yh=yl, yl=yh))
            elif PATH[g] == "c":
                send(*args, dev(z=zz, yl=1 - yl))
            elif dz != 0:
                send(*args, dev(z=zz))
    send(a_ref, afull.at[h], a_sem.at[1], a_sem.at[2], dev(h=1 - h))

    def over_x(g):
        path = PATH[g]
        nyh, nyl = {"a": (yh, yl), "b": (yl, yh), "c": (1 - yl, 1 - yh)}[path]
        same_y = {"a": True, "b": yl == yh, "c": yl != yh}[path]
        for k in (0, 1, 3, 2):
            if path == "b" and k == 0:
                src = piece(z, g)
            else:
                src = tz.at[g, k]
                arrive(src, tz_r.at[g, k])
            xd = (z + k) % 4
            slot = (x + 4 - xd) % 4
            dst = m.at[pl.ds(pl.multiple_of(g * SUB + slot * CH, CH), CH)]
            here = jnp.logical_and(same_y, xd == x)
            send_unless(here, src, dst, tx_s.at[g, k], tx_r.at[g], dev(x=xd, yh=nyh, yl=nyl))

    def msub(s, lo=0, n=SUB):
        return m.at[s * SUB + lo:s * SUB + lo + n]

    def multiply(s0, n):
        rows = slice(s0 * SUB, (s0 + n) * SUB)

        for hf in range(2):

            def tile(it, carry):
                col_at = pl.ds(pl.multiple_of(it * TILE, TILE), TILE)
                at = pl.ds(pl.multiple_of(hf * HALF + it * TILE, TILE), TILE)
                dims = (((1,), (1,)), ((), ()))
                acc = lax.dot_general(m[rows, :HALF], afull[0, at, :], dims, preferred_element_type=F32)
                acc += lax.dot_general(m[rows, HALF:], afull[1, at, :], dims, preferred_element_type=F32)
                for i in range(n):
                    at_row = slice((s0 + i) * CH, (s0 + i + 1) * CH)
                    pown[at_row, at] = acc[i * SUB:i * SUB + CH]
                    for k in range(3):
                        lo = i * SUB + (k + 1) * CH
                        p[k, hf, at_row, col_at] = acc[lo:lo + CH].astype(BF)
                return carry

            lax.fori_loop(0, HALF // TILE, tile, 0)

    half = (slice(0, HALF), slice(HALF, ROWS))

    def rows_of(b):
        s0, n = UNITS[b]
        return slice(s0 * CH, (s0 + n) * CH)

    def x_send(b, i, src, dst, to):
        send(src, dst, rs_s.at[b, i], rs_r.at[b, i], to)

    def reduce_1(b):
        r = rows_of(b)
        x_send(b, 0, p.at[1, 0, r], ra.at[r], dev(x=xp))
        x_send(b, 1, p.at[1, 1, r], rb.at[r], dev(x=xm))
        x_send(b, 2, p.at[0, 1, r], db.at[r], dev(x=xp))
        x_send(b, 3, p.at[2, 0, r], da.at[r], dev(x=xm))

    def reduce_2(b):
        r = rows_of(b)
        arrive(ra.at[r], rs_r.at[b, 0])
        p[0, 0, r] = (p[0, 0, r].astype(F32) + ra[r].astype(F32)).astype(BF)
        x_send(b, 4, p.at[0, 0, r], ea.at[r], dev(x=xp))
        arrive(rb.at[r], rs_r.at[b, 1])
        p[2, 1, r] = (p[2, 1, r].astype(F32) + rb[r].astype(F32)).astype(BF)
        x_send(b, 5, p.at[2, 1, r], eb.at[r], dev(x=xm))

    def mine(g):
        return (yl + FLIP[g] + yh) % 2

    def reduce_3(b):
        r = rows_of(b)
        arrive(db.at[r], rs_r.at[b, 2])
        arrive(da.at[r], rs_r.at[b, 3])
        arrive(ea.at[r], rs_r.at[b, 4])
        arrive(eb.at[r], rs_r.at[b, 5])
        s0, n = UNITS[b]
        pairs = []
        for s in range(s0, s0 + n):
            kind, fam, g = SHARDS[s]
            pair = kind * GROUPS + g
            r = slice(s * CH, (s + 1) * CH)
            s2[pair, fam, :, half[0]] = pown[r, half[0]] + (ea[r].astype(F32) + da[r].astype(F32))
            s2[pair, fam, :, half[1]] = pown[r, half[1]] + (eb[r].astype(F32) + db[r].astype(F32))
            if fam == 1:
                ysend[pair] = s2[pair, 1 - mine(g)].astype(BF)
                send(ysend.at[pair], yrecv.at[pair], y_s.at[pair], y_r.at[pair], dev(yh=1 - yh))
                pairs.append(pair)
        return pairs

    def finish(pair):
        kind, g = pair // GROUPS, pair % GROUPS
        arrive(yrecv.at[pair], y_r.at[pair])
        total = s2[pair, mine(g)] + yrecv[pair].astype(F32)
        zz = (z + ZOFF[kind]) % 4
        at = pl.ds(pl.multiple_of(zz * 64 + g * CH, CH), CH)
        u_ref[at, :] = (-total * mask[0:1, :]).astype(BF)
        copy = pltpu.make_async_copy(u_ref.at[at], u_hbm.at[at], u_sem.at[pair])
        copy.start()
        stores.append(copy)

    def m_send(s, to, at, sem=None, lo=0, n=SUB):
        sem = at if sem is None else sem
        send(msub(s, lo, n), msub(at, lo, n), m_s.at[sem], m_r.at[sem], to)

    def arrival(what, g):
        s = BASE[what, g]
        if what == "own":
            to = BASE["near", g]
            arrive(msub(s), tx_r.at[g])
            m_send(s, dev(z=zp), to)
            m_send(s, dev(z=zm), to + 1)
            m_send(s, dev(yl=1 - yl), to + 2)
        elif what == "near":
            two, to = BASE["two", g], BASE["far", g]
            for i in range(3):
                arrive(msub(s + i), m_r.at[s + i])
            m_send(s, dev(z=zp), two, two, 0, SUB // 2)
            m_send(s + 1, dev(z=zm), two, NSUB + g, SUB // 2, SUB // 2)
            m_send(s + 2, dev(z=zp), to)
            m_send(s + 2, dev(z=zm), to + 1)
        elif what == "two":
            arrive(msub(s, 0, SUB // 2), m_r.at[s])
            arrive(msub(s, SUB // 2, SUB // 2), m_r.at[NSUB + g])
            m_send(s, dev(yl=1 - yl), BASE["far", g] + 2)
        else:
            for i in range(3):
                arrive(msub(s + i), m_r.at[s + i])

    def others():
        for k in range(1, 8):
            r = (row + k) % 8
            yield k, r, (r, col)

    def correction(parts):
        rows = jnp.concatenate([u_ref[lo:lo + n] for lo, n in parts], axis=0)
        return lax.dot_general(rows, mt[...], (((1,), (1,)), ((), ())), preferred_element_type=F32)

    def share(r):
        return pl.ds(pl.multiple_of(r * 24, 8), 24)

    def send_early():
        early[...] = correction([(zz * 64, 48) for zz in range(4)])
        for k, r, to in others():
            send(early.at[share(r)], early_in.at[8 - k], d_s.at[0, k], d_r.at[0, 8 - k], to)

    def sum_early():
        total = early[share(row), :]
        for k in range(1, 8):
            arrive(early_in.at[k], d_r.at[0, k])
            total += early_in[k]
        early_in[0] = total
        for k, r, to in others():
            send(early_in.at[0], early_sum.at[row], d_s.at[1, k], d_r.at[1, 8 - k], to)
        early_sum[row] = total

    def arrive_early():
        for k, r, to in others():
            arrive(early_sum.at[r], d_r.at[1, k])
        for zz in range(4):
            for i in range(2):
                lo = zz * 64 + i * 24
                corr[lo:lo + 24] = early_sum[zz * 2 + i]

    ready = {}
    drained = marked = 0
    for what, arg in schedule():
        if what == "over_x":
            over_x(arg)
        elif what == "swap":
            a_local.wait()
            arrive(afull.at[1 - h], a_sem.at[2])
        elif what == "mul":
            multiply(*arg)
        elif what == "r1":
            reduce_1(arg)
        elif what == "r2":
            reduce_2(arg)
        elif what == "r3":
            ready[arg] = reduce_3(arg)
        elif what == "mark":
            marked = len(sends)
        elif what == "drain":
            for copy in sends[drained:marked]:
                copy.wait_send()
            drained = marked
            for here, remote_copy in tx_waits:
                wait_unless(here, remote_copy)
            tx_waits.clear()
        elif what == "send_early":
            send_early()
        elif what == "sum_early":
            sum_early()
        elif what == "fin":
            for pair in ready[arg]:
                finish(pair)
        else:
            arrival(what, arg)

    late[row] = correction([(zz * 64 + 48, CH) for zz in range(4)]).astype(BF)
    for k, r, to in others():
        send(late.at[row], late.at[row], d_s.at[2, k], d_r.at[2, 8 - k], to)
    arrive_early()
    for k, r, to in others():
        arrive(late.at[r], d_r.at[2, k])
    total = late[0].astype(F32)
    for r in range(1, 8):
        total += late[r].astype(F32)
    for zz in range(4):
        corr[zz * 64 + 48:(zz + 1) * 64] = total[zz * CH:(zz + 1) * CH]
    dinv_copy.wait()
    diag_ref[0] = dinv_ref[0] - corr[...].T
    copy = pltpu.make_async_copy(diag_ref, diag_hbm, io_sem.at[2])
    copy.start()
    stores.append(copy)

    for copy in stores:
        copy.wait()
    for copy in sends[drained:]:
        copy.wait_send()


def place(u_in, diag_in, u_out, diag_out):
    u_out[...] = u_in[...]
    diag_out[...] = diag_in[...]


def local(inverse_anc, factor_panel, pattern, diag_inverse):
    hbm = pl.BlockSpec(memory_space=pl.ANY)
    dma = pltpu.SemaphoreType.DMA
    blocks = [pl.BlockSpec((128, ROWS), lambda i: (i, 0)), pl.BlockSpec((1, 128, SUPER), lambda i: (0, i, 0))]
    part = pltpu.VMEM((NSUB * CH, HALF), BF)
    out = pl.pallas_call(
        kernel,
        out_shape=(
            jax.ShapeDtypeStruct((SUPER, ROWS), BF),
            jax.ShapeDtypeStruct((1, SUPER, SUPER), F32),
        ),
        in_specs=[hbm, hbm, pl.BlockSpec(memory_space=pltpu.SMEM), hbm],
        out_specs=(hbm, hbm),
        scratch_shapes=[
            pltpu.VMEM((ROWS, SUPER), BF),
            pltpu.VMEM((1, SUPER, SUPER), F32),
            pltpu.VMEM((SUPER, ROWS), BF),
            pltpu.VMEM((1, SUPER, SUPER), F32),
            pltpu.VMEM((2, ROWS, HALF), BF),
            pltpu.VMEM((SUPER, ROWS), BF),
            pltpu.VMEM((8, ROWS), F32),
            pltpu.VMEM((GROUPS, 4, CH, ROWS), BF),
            pltpu.VMEM((NSUB * SUB, ROWS), BF),
            pltpu.VMEM((3, 2, NSUB * CH, HALF), BF),
            pltpu.VMEM((NSUB * CH, ROWS), F32),
            part, part, part, part, part, part,
            pltpu.VMEM((4 * GROUPS, 2, CH, ROWS), F32),
            pltpu.VMEM((4 * GROUPS, CH, ROWS), BF),
            pltpu.VMEM((4 * GROUPS, CH, ROWS), BF),
            pltpu.VMEM((192, SUPER), F32),
            pltpu.VMEM((8, 24, SUPER), F32),
            pltpu.VMEM((8, 24, SUPER), F32),
            pltpu.VMEM((8, 64, SUPER), BF),
            pltpu.VMEM((SUPER, SUPER), F32),
            dma((3,)), dma((4 * GROUPS,)),
            dma((3,)),
            dma((GROUPS, 4)), dma((GROUPS, 4)),
            dma((GROUPS, 4)), dma((GROUPS,)),
            dma((NSUB + GROUPS,)), dma((NSUB + GROUPS,)),
            dma((len(UNITS), 6)), dma((len(UNITS), 6)),
            dma((4 * GROUPS,)), dma((4 * GROUPS,)),
            dma((3, 8)), dma((3, 8)),
        ],
        compiler_params=pltpu.CompilerParams(
            collective_id=0, has_side_effects=True, vmem_limit_bytes=60 << 20
        ),
        cost_estimate=pl.CostEstimate(flops=2 * 2048 * 2048 * 2048, bytes_accessed=8 << 20, transcendentals=0),
        name="selected_inverse",
    )(inverse_anc, factor_panel, pattern, diag_inverse)
    return pl.pallas_call(
        place,
        out_shape=tuple(jax.ShapeDtypeStruct(o.shape, o.dtype) for o in out),
        grid=(2,),
        in_specs=blocks,
        out_specs=tuple(blocks),
        name="place_outputs",
    )(*out)


def solution(mesh):
    return jax.shard_map(
        local,
        mesh=mesh,
        in_specs=(P("row", "col"), P("row", "col"), P(), P("col", None, None)),
        out_specs=(P("col", "row"), P("col", None, None)),
        check_vma=False,
    )
```
